32 devices in a mesh: groups: 2 (over y), sector: 4 (over z), op: 4 (over x, core).
Axes of the slice: x: 2, y: 2, z: 4, core: 2. Of those that a mesh axis runs over, the one named last changes fastest.
Arguments:
- psi: float32 [32, 256, 256], P(('groups', 'sector')), parts along dimension 0, may hold values from -6 to 6
- left_env: float32 [40, 32, 256, 256], P('op', ('groups', 'sector')), parts along dimension 1, may hold values from -0.375 to 0.375
- right_env: float32 [40, 32, 256, 256], P('op', ('groups', 'sector')), parts along dimension 1, may hold values from -0.375 to 0.375
- source: int32 [40, 32], P(None, 'groups'), parts along dimension 1, may hold values from 0 to 15, as said below
- coef_index: int32 [40, 32], P('op', ('groups', 'sector')), parts along dimension 1, may hold values from 0 to 23
- coef_table: float32 [24], replicated, may hold values from 0.1 to 0.3
Outputs:
- h_psi: float32 [32, 256, 256], P(('groups', 'sector'), 'op'), parts along dimension 0
The draws below stay inside these ranges and needn't reach their ends.
There are 2 independent parts, one for each index of `groups`. The reference program is written for one: setup_inputs(seed, part) draws one part's arguments, and reference() takes and returns one part's arrays. A program takes and returns all parts, laid end to end along the dimension named above; an argument that names none is the same for every part. Nothing has to cross between parts.
Inputs may be any that keep to these rules, and one draw needn't show every extreme that they name: For each block of 10 consecutive terms and each block of 4 consecutive target sectors, at most 10 of these pairs read a source sector from any one block of 4 consecutive sectors, and some such block is read exactly 10 times.
All inputs are finite; a program needn't handle non-finite values.
Results may differ from the reference program's by a relative error of at most 0.0003.
Values sent between devices are 32-bit elements; how exact they have to be, the bound alone decides.
A program may use at most 128 MiB of HBM per device.

```python
import jax
import jax.numpy as jnp
from jax import lax

BLOCK = 256
TERMS = 40
NCOEF = 24
SEC_DEV = 4
SECTORS = 16
TERM_DEV = 10
PAIRS = 40
CAP = 10
N_SECTOR = 4
N_OP = 4


def draw_source(key, part):
    key = jax.random.fold_in(key, 11)

    def one_device(sub):
        first, second = jax.random.split(sub)
        slots = jnp.arange(N_SECTOR * CAP, dtype=jnp.int32) // CAP
        owners = jax.random.permutation(first, slots)[:PAIRS]
        inner = jax.random.randint(second, (PAIRS,), 0, SEC_DEV)
        return owners * SEC_DEV + inner
    flat = jax.vmap(one_device)(jax.random.split(key, N_SECTOR * N_OP))
    grid = flat.reshape(N_SECTOR, N_OP, TERM_DEV, SEC_DEV)
    return grid.transpose(1, 2, 0, 3).reshape(TERMS, SECTORS).astype(jnp.int32)


def plant(drawn, own_key, low, high):
    shape = drawn.shape
    index_at = [jax.random.randint(jax.random.fold_in(own_key, axis), (), 0, shape[axis]) for axis in range(len(shape))]
    drawn = drawn.at[tuple(index_at)].set(low)
    longest = shape.index(max(shape))
    index_at[longest] = (index_at[longest] + 1) % shape[longest]
    return drawn.at[tuple(index_at)].set(high)


def shard_levels(rng, shape, pieces, least, high):
    factor_of = 1.0
    for position, shards_of in pieces:
        heights = jax.random.uniform(jax.random.fold_in(jax.random.fold_in(rng, 6), position), (shards_of,), jnp.float32, least / len(pieces), high / len(pieces))
        factor_of = factor_of * jnp.repeat(jnp.exp(heights), shape[position] // shards_of).reshape((-1,) + (1,) * (len(shape) - 1 - position))
    return factor_of


def centred(own_key, dims, spread, reach, cuts=(), kind=jnp.bfloat16):
    drawn = jax.random.normal(own_key, dims, jnp.float32) * spread
    if len(cuts) > 0:
        drawn = shard_levels(own_key, dims, cuts, -0.22, 0.18) * drawn
    return jnp.clip(drawn, min=-reach, max=reach).astype(kind)


def setup_inputs(seed: int = 0, part: int = 0) -> dict:
    seeds = jax.random.split(jax.random.key(seed), 7)
    own_keys = jax.random.split(jax.random.fold_in(seeds[6], part), 7)
    psi = centred(own_keys[0], (SECTORS, BLOCK, BLOCK), 1.0, 6.0, ((0, 4),), jnp.float32)
    left_env = centred(own_keys[1], (TERMS, SECTORS, BLOCK, BLOCK), BLOCK ** -0.5, 0.375, ((0, 4), (1, 4)), jnp.float32)
    right_env = centred(own_keys[2], (TERMS, SECTORS, BLOCK, BLOCK), BLOCK ** -0.5, 0.375, ((0, 4), (1, 4)), jnp.float32)
    source = draw_source(jax.random.fold_in(jax.random.fold_in(seeds[6], part), 71), part)
    coef_index = plant(jax.random.randint(own_keys[4], (TERMS, SECTORS), 0, NCOEF), jax.random.fold_in(own_keys[4], 1), 0, NCOEF - 1).astype(jnp.int32)
    coef_table = jnp.clip(jax.random.uniform(seeds[5], (NCOEF,), jnp.float32, 0.1, 0.3), 0.1, 0.3)
    return dict(psi=psi, left_env=left_env, right_env=right_env, source=source, coef_index=coef_index, coef_table=coef_table)


def reference(psi, left_env, right_env, source, coef_index, coef_table):
    levels = jnp.arange(coef_table.shape[0], dtype=jnp.int32)
    coef = jnp.sum(jnp.where(coef_index[..., None] == levels, coef_table, jnp.zeros_like(coef_table)), axis=-1)

    def one_term(carry, inputs):
        left, right, src, scale = inputs
        blocks = jnp.take(psi, src.astype(jnp.int32), axis=0)
        partial_value = jnp.einsum("sab,sbc->sac", blocks, right, precision=lax.Precision.HIGHEST) * scale[:, None, None]
        return carry + jnp.einsum("srk,skc->src", left, partial_value, precision=lax.Precision.HIGHEST), None

    total, _ = lax.scan(one_term, jnp.zeros_like(psi), (left_env, right_env, source, coef))
    return total
```

```python
import functools

import jax
import jax.numpy as jnp
from jax import lax
from jax.experimental import pallas as pl
from jax.experimental.pallas import tpu as pltpu
from jax.sharding import PartitionSpec as P

F32 = jnp.float32
BF16 = jnp.bfloat16
MESH = pl.DeviceIdType.MESH


def split(value):
    high = value.astype(BF16)
    return high, (value - high.astype(F32)).astype(BF16)


def dot3(a_hi, a_lo, b_hi, b_lo):
    dot = functools.partial(jnp.dot, preferred_element_type=F32)
    return dot(a_hi, b_hi) + dot(a_hi, b_lo) + dot(a_lo, b_hi)


def kernel(nz, nx, cap, parts, order_ref, inner_ref, coef_ref, slot_ref, psi_ref, left_ref, right_ref, out_ref,
           psi_all, left, right, cur_hi, cur_lo, par_hi, par_lo, h, first, summed, second,
           load_sem, recv_sem, z_sem, x_sem, c_sem, r1_send, r1_recv, r2_send, r2_recv):
    sec = psi_ref.shape[0]
    block = psi_ref.shape[1]
    terms = left_ref.shape[0]
    nop = 2 * nx
    rows = block // nop
    part = sec // parts
    z = lax.axis_index("sector")
    o = lax.axis_index("op")
    x = o // 2
    c = lax.rem(o, 2)
    mate = 2 * x + 1 - c

    load_psi = pltpu.make_async_copy(psi_ref, psi_all.at[z], load_sem.at[0])
    load_right = pltpu.make_async_copy(right_ref, right, load_sem.at[1])
    load_left = pltpu.make_async_copy(left_ref, left, load_sem.at[2])
    load_psi.start()
    load_right.start()
    load_left.start()

    def other(step):
        return lax.rem(x + step, nx)

    barrier = pltpu.get_barrier_semaphore()

    @pl.when(z > 0)
    def _():
        pl.semaphore_signal(barrier, inc=1, device_id={"sector": z - 1}, device_id_type=MESH)

    @pl.when(z < nz - 1)
    def _():
        pl.semaphore_signal(barrier, inc=1, device_id={"sector": z + 1}, device_id_type=MESH)

    pl.semaphore_signal(barrier, inc=1, device_id={"op": mate}, device_id_type=MESH)
    for step in range(1, nx):
        pl.semaphore_signal(barrier, inc=1, device_id={"op": 2 * other(step) + c}, device_id_type=MESH)

    inside = jnp.logical_and(z > 0, z < nz - 1)

    @pl.when(inside)
    def _():
        pl.semaphore_wait(barrier, nx + 2)

    @pl.when(jnp.logical_not(inside))
    def _():
        pl.semaphore_wait(barrier, nx + 1)

    def piece(k, i, q):
        return psi_all.at[k, pl.ds(i * part, part), pl.ds(pl.multiple_of(q * rows, rows), rows), :]

    def send(k, i, q, sem, device):
        return pltpu.make_async_remote_copy(
            src_ref=piece(k, i, q), dst_ref=piece(k, i, q), send_sem=sem, recv_sem=recv_sem.at[k, i, q],
            device_id=device, device_id_type=MESH)

    def z_copy(k, i, way):
        return send(k, i, o, z_sem.at[(way + 1) // 2, k, i], {"sector": z + way})

    def x_copy(k, i, step):
        return send(k, i, o, x_sem.at[k, i, step], {"op": 2 * other(step) + c})

    def c_copy(k, i, xq):
        return send(k, i, 2 * xq + c, c_sem.at[k, i, xq], {"op": mate})

    def arrived(k, i, q):
        send(k, i, q, z_sem.at[0, k, i], {"op": mate}).wait_recv()

    load_psi.wait()
    for i in range(parts):
        for way in (-1, 1):
            @pl.when(jnp.logical_and(z + way >= 0, z + way < nz))
            def _():
                z_copy(z, i, way).start()

    def products(k):
        def halve(s, carry):
            cur_hi[s], cur_lo[s] = split(psi_all[k, s])
            return carry
        lax.fori_loop(0, sec, halve, 0)

        def pair(j, carry):
            at = k * cap + j
            p = order_ref[at]
            s = inner_ref[at]
            r_hi, r_lo = split(right[p // sec, lax.rem(p, sec)])
            value = dot3(cur_hi[s], cur_lo[s], r_hi, r_lo) * coef_ref[at]
            par_hi[at], par_lo[at] = split(value)
            return carry
        lax.fori_loop(0, cap, pair, 0)

    load_right.wait()
    products(z)

    def both(d, body):
        for side in (-1, 1):
            k = z + side * d
            @pl.when(jnp.logical_and(d >= 1, jnp.logical_and(d < nz, jnp.logical_and(k >= 0, k < nz))))
            def _():
                body(k, side)

    def take_z(i):
        def body(k, side):
            arrived(k, i, o)
            ahead = z - side

            @pl.when(jnp.logical_and(ahead >= 0, ahead < nz))
            def _():
                z_copy(k, i, -side).start()
            for step in range(1, nx):
                x_copy(k, i, step).start()
            c_copy(k, i, x).start()
        return body

    def take_x(i):
        def body(k, side):
            for step in range(1, nx):
                arrived(k, i, 2 * other(step) + c)
                c_copy(k, i, other(step)).start()
        return body

    def take_all(k, side):
        for i in range(parts):
            for xq in range(nx):
                arrived(k, i, 2 * xq + 1 - c)
        products(k)

    def stage(d, carry):
        for i in range(parts):
            both(d, take_z(i))
            both(d - 1, take_x(i))
        both(d - 2, take_all)
        return carry
    lax.fori_loop(1, nz + 2, stage, 0)

    load_left.wait()

    def mine(t, xq, core):
        return h.at[t, pl.ds(pl.multiple_of((2 * xq + core) * rows, rows), rows), :]

    def r1_copy(t, xq):
        return pltpu.make_async_remote_copy(
            src_ref=mine(t, xq, 1 - c), dst_ref=first.at[t, xq], send_sem=r1_send.at[t, xq],
            recv_sem=r1_recv.at[t, xq], device_id={"op": mate}, device_id_type=MESH)

    def r2_copy(t, step):
        return pltpu.make_async_remote_copy(
            src_ref=summed.at[t, other(step)], dst_ref=second.at[t, step], send_sem=r2_send.at[t, step],
            recv_sem=r2_recv.at[t, step], device_id={"op": 2 * other(step) + c}, device_id_type=MESH)

    def target(t, carry):
        @pl.when(t < sec)
        def _():
            def term(w, carry):
                slot = slot_ref[w * sec + t]
                l_hi, l_lo = split(left[w, t])
                value = dot3(l_hi, l_lo, par_hi[slot], par_lo[slot])

                @pl.when(w == 0)
                def _():
                    h[t] = value

                @pl.when(w > 0)
                def _():
                    h[t] = h[t] + value
                return carry
            lax.fori_loop(0, terms, term, 0)
            for xq in range(nx):
                r1_copy(t, xq).start()

        @pl.when(t >= 1)
        def _():
            b = t - 1
            for xq in range(nx):
                r1_copy(b, xq).wait_recv()
                summed[b, xq] = mine(b, xq, c)[...] + first[b, xq]
            for step in range(1, nx):
                r2_copy(b, step).start()
        return carry
    lax.fori_loop(0, sec + 1, target, 0)

    def finish(t, carry):
        total = summed[t, x]
        for step in range(1, nx):
            r2_copy(t, step).wait_recv()
            total = total + second[t, step]
        out_ref[t] = total
        for step in range(1, nx):
            r2_copy(t, step).wait_send()
        for xq in range(nx):
            r1_copy(t, xq).wait_send()
        return carry
    lax.fori_loop(0, sec, finish, 0)

    for i in range(parts):
        for way in (-1, 1):
            @pl.when(jnp.logical_and(z + way >= 0, z + way < nz))
            def _():
                z_copy(z, i, way).wait_send()

    def drain(i):
        def body(k, side):
            ahead = z - side

            @pl.when(jnp.logical_and(ahead >= 0, ahead < nz))
            def _():
                z_copy(k, i, -side).wait_send()
            for step in range(1, nx):
                x_copy(k, i, step).wait_send()
            for xq in range(nx):
                c_copy(k, i, xq).wait_send()
        return body

    def last(d, carry):
        for i in range(parts):
            both(d, drain(i))
        return carry
    lax.fori_loop(1, nz, last, 0)


def on_device(nz, nop, psi, left_env, right_env, source, coef_index, coef_table):
    sec, block, _ = psi.shape
    terms = left_env.shape[0]
    pairs = terms * sec
    cap = -(-pairs // nz)
    slots = cap * nz
    nx = nop // 2
    rows = block // nop
    parts = 2
    my_sec = lax.axis_index("sector")
    my_op = lax.axis_index("op")
    src = lax.dynamic_slice(source, (my_op * terms, my_sec * sec), (terms, sec)).reshape(-1)
    owner = src // sec
    index = jnp.arange(pairs, dtype=jnp.int32)
    earlier = (owner[None, :] == owner[:, None]) & (index[None, :] < index[:, None])
    slot = owner * cap + jnp.sum(earlier, axis=1, dtype=jnp.int32)
    hit = slot[None, :] == jnp.arange(slots, dtype=jnp.int32)[:, None]
    order = jnp.sum(jnp.where(hit, index[None, :], 0), axis=1, dtype=jnp.int32)
    inner = jnp.sum(jnp.where(hit, (src % sec)[None, :], 0), axis=1, dtype=jnp.int32)
    levels = jnp.arange(coef_table.shape[0], dtype=jnp.int32)
    coef = jnp.sum(
        jnp.where(coef_index.reshape(-1)[:, None] == levels, coef_table, jnp.zeros_like(coef_table)), axis=-1
    )
    coef = jnp.sum(jnp.where(hit, coef[None, :], 0.0), axis=1)
    dma = pltpu.SemaphoreType.DMA
    smem = pl.BlockSpec(memory_space=pltpu.SMEM)
    hbm = pl.BlockSpec(memory_space=pl.ANY)
    return pl.pallas_call(
        functools.partial(kernel, nz, nx, cap, parts),
        out_shape=jax.ShapeDtypeStruct((sec, rows, block), F32),
        in_specs=[smem] * 4 + [hbm] * 3,
        out_specs=pl.BlockSpec(memory_space=pltpu.VMEM),
        scratch_shapes=[
            pltpu.VMEM((nz, sec, block, block), F32),
            pltpu.VMEM((terms, sec, block, block), F32),
            pltpu.VMEM((terms, sec, block, block), F32),
            pltpu.VMEM((sec, block, block), BF16),
            pltpu.VMEM((sec, block, block), BF16),
            pltpu.VMEM((slots, block, block), BF16),
            pltpu.VMEM((slots, block, block), BF16),
            pltpu.VMEM((sec, block, block), F32),
            pltpu.VMEM((sec, nx, rows, block), F32),
            pltpu.VMEM((sec, nx, rows, block), F32),
            pltpu.VMEM((sec, nx, rows, block), F32),
            dma((3,)),
            dma((nz, parts, nop)),
            dma((2, nz, parts)),
            dma((nz, parts, nx)),
            dma((nz, parts, nx)),
            dma((sec, nx)),
            dma((sec, nx)),
            dma((sec, nx)),
            dma((sec, nx)),
        ],
        compiler_params=pltpu.CompilerParams(
            collective_id=0, has_side_effects=True, vmem_limit_bytes=56 * 1024 * 1024
        ),
        cost_estimate=pl.CostEstimate(
            flops=12 * pairs * block ** 3, bytes_accessed=8 * pairs * block * block, transcendentals=0
        ),
    )(order, inner, coef, slot, psi, left_env, right_env)


def solution(mesh):
    return jax.shard_map(
        functools.partial(on_device, mesh.shape["sector"], mesh.shape["op"]),
        mesh=mesh,
        in_specs=(
            P(("groups", "sector"), None, None),
            P("op", ("groups", "sector"), None, None),
            P("op", ("groups", "sector"), None, None),
            P(None, "groups"),
            P("op", ("groups", "sector")),
            P(),
        ),
        out_specs=P(("groups", "sector"), "op", None),
        check_vma=False,
    )
```

```python
import functools

import jax
import jax.numpy as jnp
from jax import lax
from jax.experimental import pallas as pl
from jax.experimental.pallas import tpu as pltpu
from jax.sharding import PartitionSpec as P

F32 = jnp.float32
BF16 = jnp.bfloat16
MESH = pl.DeviceIdType.MESH


def split(value):
    high = value.astype(BF16)
    return high, (value - high.astype(F32)).astype(BF16)


def dot3(a_hi, a_lo, b_hi, b_lo):
    dot = functools.partial(jnp.dot, preferred_element_type=F32)
    return dot(a_hi, b_hi) + dot(a_hi, b_lo) + dot(a_lo, b_hi)


def kernel(nz, nx, cap, parts, source_ref, index_ref, table_ref, psi_ref, left_ref, right_ref, out_ref,
           after, rank, reads, psi_all, left, right, cur_hi, cur_lo, contrib, h, first, summed, second,
           load_sem, recv_sem, z_sem, x_sem, c_sem, r1_send, r1_recv, r2_send, r2_recv):
    sec = psi_ref.shape[0]
    block = psi_ref.shape[1]
    terms = left_ref.shape[0]
    nop = 2 * nx
    pairs = terms * sec
    rows = block // nop
    part = sec // parts
    z = lax.axis_index("sector")
    o = lax.axis_index("op")
    x = o // 2
    c = lax.rem(o, 2)
    mate = 2 * x + 1 - c

    load_psi = pltpu.make_async_copy(psi_ref, psi_all.at[z], load_sem.at[0])
    load_right = pltpu.make_async_copy(right_ref, right, load_sem.at[1])
    load_left = pltpu.make_async_copy(left_ref, left, load_sem.at[2])
    load_psi.start()
    load_right.start()
    load_left.start()

    def other(step):
        return lax.rem(x + step, nx)

    barrier = pltpu.get_barrier_semaphore()

    @pl.when(z > 0)
    def _():
        pl.semaphore_signal(barrier, inc=1, device_id={"sector": z - 1}, device_id_type=MESH)

    @pl.when(z < nz - 1)
    def _():
        pl.semaphore_signal(barrier, inc=1, device_id={"sector": z + 1}, device_id_type=MESH)

    pl.semaphore_signal(barrier, inc=1, device_id={"op": mate}, device_id_type=MESH)
    for step in range(1, nx):
        pl.semaphore_signal(barrier, inc=1, device_id={"op": 2 * other(step) + c}, device_id_type=MESH)

    inside = jnp.logical_and(z > 0, z < nz - 1)

    @pl.when(inside)
    def _():
        pl.semaphore_wait(barrier, nx + 2)

    @pl.when(jnp.logical_not(inside))
    def _():
        pl.semaphore_wait(barrier, nx + 1)

    def piece(k, i, q):
        return psi_all.at[k, pl.ds(i * part, part), pl.ds(pl.multiple_of(q * rows, rows), rows), :]

    def send(k, i, q, sem, device):
        return pltpu.make_async_remote_copy(
            src_ref=piece(k, i, q), dst_ref=piece(k, i, q), send_sem=sem, recv_sem=recv_sem.at[k, i, q],
            device_id=device, device_id_type=MESH)

    def z_copy(k, i, way):
        return send(k, i, o, z_sem.at[(way + 1) // 2, k, i], {"sector": z + way})

    def x_copy(k, i, step):
        return send(k, i, o, x_sem.at[k, i, step], {"op": 2 * other(step) + c})

    def c_copy(k, i, xq):
        return send(k, i, 2 * xq + c, c_sem.at[k, i, xq], {"op": mate})

    def arrived(k, i, q):
        send(k, i, q, z_sem.at[0, k, i], {"op": mate}).wait_recv()

    load_psi.wait()
    for i in range(parts):
        for way in (-1, 1):
            @pl.when(jnp.logical_and(z + way >= 0, z + way < nz))
            def _():
                z_copy(z, i, way).start()

    def source_of(p):
        return source_ref[o * terms + lax.div(p, sec), z * sec + lax.rem(p, sec)]

    def clear(p, carry):
        rank[p] = 0
        return carry
    lax.fori_loop(0, pairs, clear, 0)

    def chain(k):
        def backward(step, carry):
            found, count = carry
            p = pairs - 1 - step
            hit = lax.div(source_of(p), sec) == k
            after[p] = found
            rank[p] = jnp.where(hit, count, rank[p])
            return jnp.where(hit, p, found), jnp.where(hit, count + 1, count)
        found, count = lax.fori_loop(0, pairs, backward, (0, 0))
        reads[k] = count
        return found

    def slot(p):
        owner = lax.div(source_of(p), sec)
        return owner * cap + reads[owner] - 1 - rank[p]

    def ready(k):
        def halve(s, carry):
            cur_hi[s], cur_lo[s] = split(psi_all[k, s])
            return carry
        lax.fori_loop(0, sec, halve, 0)

    def products(k, begin, end, start):
        def pair(j, p):
            w = lax.div(p, sec)
            t = lax.rem(p, sec)
            s = lax.rem(source_of(p), sec)
            r_hi, r_lo = split(right[w, t])
            value = dot3(cur_hi[s], cur_lo[s], r_hi, r_lo) * table_ref[index_ref[w, t]]
            l_hi, l_lo = split(left[w, t])
            v_hi, v_lo = split(value)
            contrib[k * cap + j] = dot3(l_hi, l_lo, v_hi, v_lo)
            return after[p]
        return lax.fori_loop(begin, end, pair, start)

    ready(z)
    head = chain(z)
    load_right.wait()
    load_left.wait()
    middle = products(z, 0, cap // 2, head)

    def both(d, body):
        for side in (-1, 1):
            k = z + side * d
            @pl.when(jnp.logical_and(d >= 1, jnp.logical_and(d < nz, jnp.logical_and(k >= 0, k < nz))))
            def _():
                body(k, side)

    def take_z(i):
        def body(k, side):
            arrived(k, i, o)
            ahead = z - side

            @pl.when(jnp.logical_and(ahead >= 0, ahead < nz))
            def _():
                z_copy(k, i, -side).start()
            for step in range(1, nx):
                x_copy(k, i, step).start()
            c_copy(k, i, x).start()
        return body

    def take_x(i):
        def body(k, side):
            for step in range(1, nx):
                arrived(k, i, 2 * other(step) + c)
                c_copy(k, i, other(step)).start()
        return body

    def take_all(k, side):
        for i in range(parts):
            for xq in range(nx):
                arrived(k, i, 2 * xq + 1 - c)
        ready(k)
        products(k, 0, cap, chain(k))

    def stage(d, carry):
        for i in range(parts):
            both(d, take_z(i))

        @pl.when(d == 1)
        def _():
            products(z, cap // 2, cap, middle)
        both(d - 1, take_all)
        for i in range(parts):
            both(d, take_x(i))
        return carry
    lax.fori_loop(1, nz, stage, 0)
    both(nz - 1, take_all)

    def mine(t, xq, core):
        return h.at[t, pl.ds(pl.multiple_of((2 * xq + core) * rows, rows), rows), :]

    def r1_copy(t, xq):
        return pltpu.make_async_remote_copy(
            src_ref=mine(t, xq, 1 - c), dst_ref=first.at[t, xq], send_sem=r1_send.at[t, xq],
            recv_sem=r1_recv.at[t, xq], device_id={"op": mate}, device_id_type=MESH)

    def r2_copy(t, step):
        return pltpu.make_async_remote_copy(
            src_ref=summed.at[t, other(step)], dst_ref=second.at[t, step], send_sem=r2_send.at[t, step],
            recv_sem=r2_recv.at[t, step], device_id={"op": 2 * other(step) + c}, device_id_type=MESH)

    def target(t, carry):
        @pl.when(t < sec)
        def _():
            total = contrib[slot(t)]
            for w in range(1, terms):
                total = total + contrib[slot(w * sec + t)]
            h[t] = total
            for xq in range(nx):
                r1_copy(t, xq).start()

        @pl.when(t >= 1)
        def _():
            b = t - 1
            for xq in range(nx):
                r1_copy(b, xq).wait_recv()
                summed[b, xq] = mine(b, xq, c)[...] + first[b, xq]
            for step in range(1, nx):
                r2_copy(b, step).start()
        return carry
    lax.fori_loop(0, sec + 1, target, 0)

    def finish(t, carry):
        total = summed[t, x]
        for step in range(1, nx):
            r2_copy(t, step).wait_recv()
            total = total + second[t, step]
        out_ref[t] = total
        for step in range(1, nx):
            r2_copy(t, step).wait_send()
        for xq in range(nx):
            r1_copy(t, xq).wait_send()
        return carry
    lax.fori_loop(0, sec, finish, 0)

    for i in range(parts):
        for way in (-1, 1):
            @pl.when(jnp.logical_and(z + way >= 0, z + way < nz))
            def _():
                z_copy(z, i, way).wait_send()

    def drain(i):
        def body(k, side):
            ahead = z - side

            @pl.when(jnp.logical_and(ahead >= 0, ahead < nz))
            def _():
                z_copy(k, i, -side).wait_send()
            for step in range(1, nx):
                x_copy(k, i, step).wait_send()
            for xq in range(nx):
                c_copy(k, i, xq).wait_send()
        return body

    def last(d, carry):
        for i in range(parts):
            both(d, drain(i))
        return carry
    lax.fori_loop(1, nz, last, 0)


def on_device(nz, nop, psi, left_env, right_env, source, coef_index, coef_table):
    sec, block, _ = psi.shape
    terms = left_env.shape[0]
    pairs = terms * sec
    cap = -(-pairs // nz)
    slots = cap * nz
    nx = nop // 2
    rows = block // nop
    parts = 2
    dma = pltpu.SemaphoreType.DMA
    smem = pl.BlockSpec(memory_space=pltpu.SMEM)
    hbm = pl.BlockSpec(memory_space=pl.ANY)
    return pl.pallas_call(
        functools.partial(kernel, nz, nx, cap, parts),
        out_shape=jax.ShapeDtypeStruct((sec, rows, block), F32),
        in_specs=[smem] * 3 + [hbm] * 3,
        out_specs=pl.BlockSpec(memory_space=pltpu.VMEM),
        scratch_shapes=[
            pltpu.SMEM((pairs,), jnp.int32),
            pltpu.SMEM((pairs,), jnp.int32),
            pltpu.SMEM((nz,), jnp.int32),
            pltpu.VMEM((nz, sec, block, block), F32),
            pltpu.VMEM((terms, sec, block, block), F32),
            pltpu.VMEM((terms, sec, block, block), F32),
            pltpu.VMEM((sec, block, block), BF16),
            pltpu.VMEM((sec, block, block), BF16),
            pltpu.VMEM((slots, block, block), F32),
            pltpu.VMEM((sec, block, block), F32),
            pltpu.VMEM((sec, nx, rows, block), F32),
            pltpu.VMEM((sec, nx, rows, block), F32),
            pltpu.VMEM((sec, nx, rows, block), F32),
            dma((3,)),
            dma((nz, parts, nop)),
            dma((2, nz, parts)),
            dma((nz, parts, nx)),
            dma((nz, parts, nx)),
            dma((sec, nx)),
            dma((sec, nx)),
            dma((sec, nx)),
            dma((sec, nx)),
        ],
        compiler_params=pltpu.CompilerParams(
            collective_id=0, has_side_effects=True, vmem_limit_bytes=56 * 1024 * 1024
        ),
        cost_estimate=pl.CostEstimate(
            flops=12 * pairs * block ** 3, bytes_accessed=8 * pairs * block * block, transcendentals=0
        ),
    )(source, coef_index, coef_table, psi, left_env, right_env)


def solution(mesh):
    return jax.shard_map(
        functools.partial(on_device, mesh.shape["sector"], mesh.shape["op"]),
        mesh=mesh,
        in_specs=(
            P(("groups", "sector"), None, None),
            P("op", ("groups", "sector"), None, None),
            P("op", ("groups", "sector"), None, None),
            P(None, "groups"),
            P("op", ("groups", "sector")),
            P(),
        ),
        out_specs=P(("groups", "sector"), "op", None),
        check_vma=False,
    )
```

```python
import functools

import jax
import jax.numpy as jnp
from jax import lax
from jax.experimental import pallas as pl
from jax.experimental.pallas import tpu as pltpu
from jax.sharding import PartitionSpec as P

F32 = jnp.float32
BF16 = jnp.bfloat16
MESH = pl.DeviceIdType.MESH


def split(value):
    high = value.astype(BF16)
    return high, (value - high.astype(F32)).astype(BF16)


def dot3(a_hi, a_lo, b_hi, b_lo):
    dot = functools.partial(jnp.dot, preferred_element_type=F32)
    return dot(a_hi, b_hi) + dot(a_hi, b_lo) + dot(a_lo, b_hi)


def kernel(nz, nx, cap, parts, source_ref, index_ref, table_ref, psi_ref, left_ref, right_ref, out_ref,
           after, rank, reads, psi_all, left, right, cur_hi, cur_lo, contrib, h, first, summed, second,
           load_sem, recv_sem, z_sem, x_sem, c_sem, r1_send, r1_recv, r2_send, r2_recv):
    sec = psi_ref.shape[0]
    block = psi_ref.shape[1]
    terms = left_ref.shape[0]
    nop = 2 * nx
    pairs = terms * sec
    rows = block // nop
    part = sec // parts
    z = lax.axis_index("sector")
    o = lax.axis_index("op")
    x = o // 2
    c = lax.rem(o, 2)
    mate = 2 * x + 1 - c

    load_psi = pltpu.make_async_copy(psi_ref, psi_all.at[z], load_sem.at[0])
    load_right = pltpu.make_async_copy(right_ref, right, load_sem.at[1])
    load_left = pltpu.make_async_copy(left_ref, left, load_sem.at[2])
    load_psi.start()
    load_right.start()
    load_left.start()

    def other(step):
        return lax.rem(x + step, nx)

    barrier = pltpu.get_barrier_semaphore()

    @pl.when(z > 0)
    def _():
        pl.semaphore_signal(barrier, inc=1, device_id={"sector": z - 1}, device_id_type=MESH)

    @pl.when(z < nz - 1)
    def _():
        pl.semaphore_signal(barrier, inc=1, device_id={"sector": z + 1}, device_id_type=MESH)

    pl.semaphore_signal(barrier, inc=1, device_id={"op": mate}, device_id_type=MESH)
    for step in range(1, nx):
        pl.semaphore_signal(barrier, inc=1, device_id={"op": 2 * other(step) + c}, device_id_type=MESH)

    inside = jnp.logical_and(z > 0, z < nz - 1)

    @pl.when(inside)
    def _():
        pl.semaphore_wait(barrier, nx + 2)

    @pl.when(jnp.logical_not(inside))
    def _():
        pl.semaphore_wait(barrier, nx + 1)

    def piece(k, i, q):
        return psi_all.at[k, pl.ds(i * part, part), pl.ds(pl.multiple_of(q * rows, rows), rows), :]

    def send(k, i, q, sem, device):
        return pltpu.make_async_remote_copy(
            src_ref=piece(k, i, q), dst_ref=piece(k, i, q), send_sem=sem, recv_sem=recv_sem.at[k, i, q],
            device_id=device, device_id_type=MESH)

    def z_copy(k, i, way):
        return send(k, i, o, z_sem.at[(way + 1) // 2, k, i], {"sector": z + way})

    def x_copy(k, i, step):
        return send(k, i, o, x_sem.at[k, i, step], {"op": 2 * other(step) + c})

    def c_copy(k, i, xq):
        return send(k, i, 2 * xq + c, c_sem.at[k, i, xq], {"op": mate})

    def arrived(k, i, q):
        send(k, i, q, z_sem.at[0, k, i], {"op": mate}).wait_recv()

    load_psi.wait()
    for i in range(parts):
        for way in (-1, 1):
            @pl.when(jnp.logical_and(z + way >= 0, z + way < nz))
            def _():
                z_copy(z, i, way).start()

    def source_of(p):
        return source_ref[o * terms + lax.div(p, sec), z * sec + lax.rem(p, sec)]

    def clear(p, carry):
        rank[p] = 0
        return carry
    lax.fori_loop(0, pairs, clear, 0)

    def chain(k):
        def backward(step, carry):
            found, count = carry
            p = pairs - 1 - step
            hit = lax.div(source_of(p), sec) == k
            after[p] = found
            rank[p] = jnp.where(hit, count, rank[p])
            return jnp.where(hit, p, found), jnp.where(hit, count + 1, count)
        found, count = lax.fori_loop(0, pairs, backward, (0, 0))
        reads[k] = count
        return found

    def slot(p):
        owner = lax.div(source_of(p), sec)
        return owner * cap + reads[owner] - 1 - rank[p]

    def ready(k):
        def halve(s, carry):
            cur_hi[s], cur_lo[s] = split(psi_all[k, s])
            return carry
        lax.fori_loop(0, sec, halve, 0)

    def products(k, begin, end, start):
        def pair(j, p):
            w = lax.div(p, sec)
            t = lax.rem(p, sec)
            s = lax.rem(source_of(p), sec)
            r_hi, r_lo = split(right[w, t])
            value = dot3(cur_hi[s], cur_lo[s], r_hi, r_lo) * table_ref[index_ref[w, t]]
            l_hi, l_lo = split(left[w, t])
            v_hi, v_lo = split(value)
            contrib[k * cap + j] = dot3(l_hi, l_lo, v_hi, v_lo)
            return after[p]
        return lax.fori_loop(begin, end, pair, start, unroll=True)

    ready(z)
    head = chain(z)
    load_right.wait()
    load_left.wait()
    middle = products(z, 0, cap // 2, head)

    def both(d, body):
        for side in (-1, 1):
            k = z + side * d
            @pl.when(jnp.logical_and(d >= 1, jnp.logical_and(d < nz, jnp.logical_and(k >= 0, k < nz))))
            def _():
                body(k, side)

    def take_z(i):
        def body(k, side):
            arrived(k, i, o)
            ahead = z - side

            @pl.when(jnp.logical_and(ahead >= 0, ahead < nz))
            def _():
                z_copy(k, i, -side).start()
            for step in range(1, nx):
                x_copy(k, i, step).start()
            c_copy(k, i, x).start()
        return body

    def take_x(i):
        def body(k, side):
            for step in range(1, nx):
                arrived(k, i, 2 * other(step) + c)
                c_copy(k, i, other(step)).start()
        return body

    def take_all(k, side):
        for i in range(parts):
            for xq in range(nx):
                arrived(k, i, 2 * xq + 1 - c)
        ready(k)
        products(k, 0, cap, chain(k))

    def stage(d, carry):
        for i in range(parts):
            both(d, take_z(i))

        @pl.when(d == 1)
        def _():
            products(z, cap // 2, cap, middle)
        for i in range(parts):
            both(d - 1, take_x(i))
        both(d - 1, take_all)
        return carry
    lax.fori_loop(1, nz + 1, stage, 0)

    def mine(t, xq, core):
        return h.at[t, pl.ds(pl.multiple_of((2 * xq + core) * rows, rows), rows), :]

    def r1_copy(t, xq):
        return pltpu.make_async_remote_copy(
            src_ref=mine(t, xq, 1 - c), dst_ref=first.at[t, xq], send_sem=r1_send.at[t, xq],
            recv_sem=r1_recv.at[t, xq], device_id={"op": mate}, device_id_type=MESH)

    def r2_copy(t, step):
        return pltpu.make_async_remote_copy(
            src_ref=summed.at[t, other(step)], dst_ref=second.at[t, step], send_sem=r2_send.at[t, step],
            recv_sem=r2_recv.at[t, step], device_id={"op": 2 * other(step) + c}, device_id_type=MESH)

    def target(t, carry):
        @pl.when(t < sec)
        def _():
            total = contrib[slot(t)]
            for w in range(1, terms):
                total = total + contrib[slot(w * sec + t)]
            h[t] = total
            for xq in range(nx):
                r1_copy(t, xq).start()

        @pl.when(t >= 1)
        def _():
            b = t - 1
            for xq in range(nx):
                r1_copy(b, xq).wait_recv()
                summed[b, xq] = mine(b, xq, c)[...] + first[b, xq]
            for step in range(1, nx):
                r2_copy(b, step).start()
        return carry
    lax.fori_loop(0, sec + 1, target, 0)

    def finish(t, carry):
        total = summed[t, x]
        for step in range(1, nx):
            r2_copy(t, step).wait_recv()
            total = total + second[t, step]
        out_ref[t] = total
        for step in range(1, nx):
            r2_copy(t, step).wait_send()
        for xq in range(nx):
            r1_copy(t, xq).wait_send()
        return carry
    lax.fori_loop(0, sec, finish, 0)

    for i in range(parts):
        for way in (-1, 1):
            @pl.when(jnp.logical_and(z + way >= 0, z + way < nz))
            def _():
                z_copy(z, i, way).wait_send()

    def drain(i):
        def body(k, side):
            ahead = z - side

            @pl.when(jnp.logical_and(ahead >= 0, ahead < nz))
            def _():
                z_copy(k, i, -side).wait_send()
            for step in range(1, nx):
                x_copy(k, i, step).wait_send()
            for xq in range(nx):
                c_copy(k, i, xq).wait_send()
        return body

    def last(d, carry):
        for i in range(parts):
            both(d, drain(i))
        return carry
    lax.fori_loop(1, nz, last, 0)


def on_device(nz, nop, psi, left_env, right_env, source, coef_index, coef_table):
    sec, block, _ = psi.shape
    terms = left_env.shape[0]
    pairs = terms * sec
    cap = -(-pairs // nz)
    slots = cap * nz
    nx = nop // 2
    rows = block // nop
    parts = 2
    dma = pltpu.SemaphoreType.DMA
    smem = pl.BlockSpec(memory_space=pltpu.SMEM)
    hbm = pl.BlockSpec(memory_space=pl.ANY)
    return pl.pallas_call(
        functools.partial(kernel, nz, nx, cap, parts),
        out_shape=jax.ShapeDtypeStruct((sec, rows, block), F32),
        in_specs=[smem] * 3 + [hbm] * 3,
        out_specs=pl.BlockSpec(memory_space=pltpu.VMEM),
        scratch_shapes=[
            pltpu.SMEM((pairs,), jnp.int32),
            pltpu.SMEM((pairs,), jnp.int32),
            pltpu.SMEM((nz,), jnp.int32),
            pltpu.VMEM((nz, sec, block, block), F32),
            pltpu.VMEM((terms, sec, block, block), F32),
            pltpu.VMEM((terms, sec, block, block), F32),
            pltpu.VMEM((sec, block, block), BF16),
            pltpu.VMEM((sec, block, block), BF16),
            pltpu.VMEM((slots, block, block), F32),
            pltpu.VMEM((sec, block, block), F32),
            pltpu.VMEM((sec, nx, rows, block), F32),
            pltpu.VMEM((sec, nx, rows, block), F32),
            pltpu.VMEM((sec, nx, rows, block), F32),
            dma((3,)),
            dma((nz, parts, nop)),
            dma((2, nz, parts)),
            dma((nz, parts, nx)),
            dma((nz, parts, nx)),
            dma((sec, nx)),
            dma((sec, nx)),
            dma((sec, nx)),
            dma((sec, nx)),
        ],
        compiler_params=pltpu.CompilerParams(
            collective_id=0, has_side_effects=True, vmem_limit_bytes=56 * 1024 * 1024
        ),
        cost_estimate=pl.CostEstimate(
            flops=12 * pairs * block ** 3, bytes_accessed=8 * pairs * block * block, transcendentals=0
        ),
    )(source, coef_index, coef_table, psi, left_env, right_env)


def solution(mesh):
    return jax.shard_map(
        functools.partial(on_device, mesh.shape["sector"], mesh.shape["op"]),
        mesh=mesh,
        in_specs=(
            P(("groups", "sector"), None, None),
            P("op", ("groups", "sector"), None, None),
            P("op", ("groups", "sector"), None, None),
            P(None, "groups"),
            P("op", ("groups", "sector")),
            P(),
        ),
        out_specs=P(("groups", "sector"), "op", None),
        check_vma=False,
    )
```

```python
import functools

import jax
import jax.numpy as jnp
from jax import lax
from jax.experimental import pallas as pl
from jax.experimental.pallas import tpu as pltpu
from jax.sharding import PartitionSpec as P

F32 = jnp.float32
BF16 = jnp.bfloat16
MESH = pl.DeviceIdType.MESH


def split(value):
    high = value.astype(BF16)
    return high, (value - high.astype(F32)).astype(BF16)


def dot3(a_hi, a_lo, b_hi, b_lo):
    dot = functools.partial(jnp.dot, preferred_element_type=F32)
    return dot(a_hi, b_hi) + dot(a_hi, b_lo) + dot(a_lo, b_hi)


def kernel(nz, nx, cap, parts, source_hbm, index_hbm, table_ref, psi_ref, left_ref, right_ref, out_ref,
           source_ref, index_ref, after, rank, reads, middle, psi_all, left, right, cur_hi, cur_lo, contrib, h, first, summed, second,
           load_sem, recv_sem, z_sem, x_sem, c_sem, r1_send, r1_recv, r2_send, r2_recv):
    sec = psi_ref.shape[0]
    block = psi_ref.shape[1]
    terms = left_ref.shape[0]
    nop = 2 * nx
    pairs = terms * sec
    rows = block // nop
    part = sec // parts
    z = lax.axis_index("sector")
    o = lax.axis_index("op")
    x = o // 2
    c = lax.rem(o, 2)
    mate = 2 * x + 1 - c

    load_psi = pltpu.make_async_copy(psi_ref, psi_all.at[z], load_sem.at[0])
    load_right = pltpu.make_async_copy(right_ref, right, load_sem.at[1])
    load_left = pltpu.make_async_copy(left_ref, left, load_sem.at[2])
    load_psi.start()
    load_source = pltpu.make_async_copy(source_hbm, source_ref, load_sem.at[3])
    load_index = pltpu.make_async_copy(index_hbm, index_ref, load_sem.at[4])
    load_source.start()
    load_index.start()

    def other(step):
        return lax.rem(x + step, nx)

    barrier = pltpu.get_barrier_semaphore()

    @pl.when(z > 0)
    def _():
        pl.semaphore_signal(barrier, inc=1, device_id={"sector": z - 1}, device_id_type=MESH)

    @pl.when(z < nz - 1)
    def _():
        pl.semaphore_signal(barrier, inc=1, device_id={"sector": z + 1}, device_id_type=MESH)

    pl.semaphore_signal(barrier, inc=1, device_id={"op": mate}, device_id_type=MESH)
    for step in range(1, nx):
        pl.semaphore_signal(barrier, inc=1, device_id={"op": 2 * other(step) + c}, device_id_type=MESH)

    inside = jnp.logical_and(z > 0, z < nz - 1)

    @pl.when(inside)
    def _():
        pl.semaphore_wait(barrier, nx + 2)

    @pl.when(jnp.logical_not(inside))
    def _():
        pl.semaphore_wait(barrier, nx + 1)

    def piece(k, i, q):
        return psi_all.at[k, pl.ds(i * part, part), pl.ds(pl.multiple_of(q * rows, rows), rows), :]

    def send(k, i, q, sem, device):
        return pltpu.make_async_remote_copy(
            src_ref=piece(k, i, q), dst_ref=piece(k, i, q), send_sem=sem, recv_sem=recv_sem.at[k, i, q],
            device_id=device, device_id_type=MESH)

    def z_copy(k, i, way):
        return send(k, i, o, z_sem.at[(way + 1) // 2, k, i], {"sector": z + way})

    def x_copy(k, i, step):
        return send(k, i, o, x_sem.at[k, i, step], {"op": 2 * other(step) + c})

    def c_copy(k, i, xq):
        return send(k, i, 2 * xq + c, c_sem.at[k, i, xq], {"op": mate})

    def arrived(k, i, q):
        send(k, i, q, z_sem.at[0, k, i], {"op": mate}).wait_recv()

    load_psi.wait()
    for i in range(parts):
        for way in (-1, 1):
            @pl.when(jnp.logical_and(z + way >= 0, z + way < nz))
            def _():
                z_copy(z, i, way).start()
    load_right.start()
    load_left.start()

    def source_of(p):
        return source_ref[z * sec + lax.rem(p, sec), o * terms + lax.div(p, sec)]

    load_source.wait()
    load_index.wait()

    def clear(p, carry):
        rank[p] = 0
        return carry
    lax.fori_loop(0, pairs, clear, 0)

    def chain(k):
        def backward(step, carry):
            found, count = carry
            p = pairs - 1 - step
            hit = lax.div(source_of(p), sec) == k
            after[p] = found
            rank[p] = jnp.where(hit, count, rank[p])
            return jnp.where(hit, p, found), jnp.where(hit, count + 1, count)
        found, count = lax.fori_loop(0, pairs, backward, (0, 0))
        reads[k] = count
        return found

    def slot(p):
        owner = lax.div(source_of(p), sec)
        return owner * cap + reads[owner] - 1 - rank[p]

    def ready(k):
        def halve(s, carry):
            cur_hi[s], cur_lo[s] = split(psi_all[k, s])
            return carry
        lax.fori_loop(0, sec, halve, 0)

    def products(k, begin, end, start):
        def pair(j, p):
            w = lax.div(p, sec)
            t = lax.rem(p, sec)
            s = lax.rem(source_of(p), sec)
            r_hi, r_lo = split(right[w, t])
            value = dot3(cur_hi[s], cur_lo[s], r_hi, r_lo) * table_ref[index_ref[t, w]]
            l_hi, l_lo = split(left[w, t])
            v_hi, v_lo = split(value)
            contrib[k * cap + j] = dot3(l_hi, l_lo, v_hi, v_lo)
            return after[p]
        return lax.fori_loop(begin, end, pair, start, unroll=True)

    ready(z)
    head = chain(z)
    def both(d, body):
        for side in (-1, 1):
            k = z + side * d
            @pl.when(jnp.logical_and(d >= 1, jnp.logical_and(d < nz, jnp.logical_and(k >= 0, k < nz))))
            def _():
                body(k, side)

    def take_z(i):
        def body(k, side):
            arrived(k, i, o)
            ahead = z - side

            @pl.when(jnp.logical_and(ahead >= 0, ahead < nz))
            def _():
                z_copy(k, i, -side).start()
            for step in range(1, nx):
                x_copy(k, i, step).start()
            c_copy(k, i, x).start()
        return body

    def take_x(i):
        def body(k, side):
            for step in range(1, nx):
                arrived(k, i, 2 * other(step) + c)
                c_copy(k, i, other(step)).start()
        return body

    def take_all(k, side):
        start = chain(k)
        for i in range(parts):
            for xq in range(nx):
                arrived(k, i, 2 * xq + 1 - c)
        ready(k)
        products(k, 0, cap, start)

    def stage(d, carry):
        for i in range(parts):
            both(d, take_z(i))

        @pl.when(d == 1)
        def _():
            load_right.wait()
            load_left.wait()
            middle[0] = products(z, 0, cap // 2, head)

        @pl.when(d == 2)
        def _():
            products(z, cap // 2, cap, middle[0])
        for i in range(parts):
            both(d - 1, take_x(i))
        both(d - 1, take_all)
        return carry
    lax.fori_loop(1, nz + 1, stage, 0)

    def mine(t, xq, core):
        return h.at[t, pl.ds(pl.multiple_of((2 * xq + core) * rows, rows), rows), :]

    def r1_copy(t, xq):
        return pltpu.make_async_remote_copy(
            src_ref=mine(t, xq, 1 - c), dst_ref=first.at[t, xq], send_sem=r1_send.at[t, xq],
            recv_sem=r1_recv.at[t, xq], device_id={"op": mate}, device_id_type=MESH)

    def r2_copy(t, step):
        return pltpu.make_async_remote_copy(
            src_ref=summed.at[t, other(step)], dst_ref=second.at[t, step], send_sem=r2_send.at[t, step],
            recv_sem=r2_recv.at[t, step], device_id={"op": 2 * other(step) + c}, device_id_type=MESH)

    def target(t, carry):
        @pl.when(t < sec)
        def _():
            total = contrib[slot(t)]
            for w in range(1, terms):
                total = total + contrib[slot(w * sec + t)]
            h[t] = total
            for xq in range(nx):
                r1_copy(t, xq).start()

        @pl.when(t >= 1)
        def _():
            b = t - 1
            for xq in range(nx):
                r1_copy(b, xq).wait_recv()
                summed[b, xq] = mine(b, xq, c)[...] + first[b, xq]
            for step in range(1, nx):
                r2_copy(b, step).start()
        return carry
    lax.fori_loop(0, sec + 1, target, 0)

    def finish(t, carry):
        total = summed[t, x]
        for step in range(1, nx):
            r2_copy(t, step).wait_recv()
            total = total + second[t, step]
        out_ref[t] = total
        for step in range(1, nx):
            r2_copy(t, step).wait_send()
        for xq in range(nx):
            r1_copy(t, xq).wait_send()
        return carry
    lax.fori_loop(0, sec, finish, 0)

    for i in range(parts):
        for way in (-1, 1):
            @pl.when(jnp.logical_and(z + way >= 0, z + way < nz))
            def _():
                z_copy(z, i, way).wait_send()

    def drain(i):
        def body(k, side):
            ahead = z - side

            @pl.when(jnp.logical_and(ahead >= 0, ahead < nz))
            def _():
                z_copy(k, i, -side).wait_send()
            for step in range(1, nx):
                x_copy(k, i, step).wait_send()
            for xq in range(nx):
                c_copy(k, i, xq).wait_send()
        return body

    def last(d, carry):
        for i in range(parts):
            both(d, drain(i))
        return carry
    lax.fori_loop(1, nz, last, 0)


def on_device(nz, nop, psi, left_env, right_env, source, coef_index, coef_table):
    sec, block, _ = psi.shape
    terms = left_env.shape[0]
    pairs = terms * sec
    cap = -(-pairs // nz)
    slots = cap * nz
    nx = nop // 2
    rows = block // nop
    parts = 1
    dma = pltpu.SemaphoreType.DMA
    smem = pl.BlockSpec(memory_space=pltpu.SMEM)
    hbm = pl.BlockSpec(memory_space=pl.ANY)
    return pl.pallas_call(
        functools.partial(kernel, nz, nx, cap, parts),
        out_shape=jax.ShapeDtypeStruct((sec, rows, block), F32),
        in_specs=[hbm] * 2 + [smem] + [hbm] * 3,
        out_specs=pl.BlockSpec(memory_space=pltpu.VMEM),
        scratch_shapes=[
            pltpu.SMEM(source.shape[::-1], jnp.int32),
            pltpu.SMEM(coef_index.shape[::-1], jnp.int32),
            pltpu.SMEM((pairs,), jnp.int32),
            pltpu.SMEM((pairs,), jnp.int32),
            pltpu.SMEM((nz,), jnp.int32),
            pltpu.SMEM((1,), jnp.int32),
            pltpu.VMEM((nz, sec, block, block), F32),
            pltpu.VMEM((terms, sec, block, block), F32),
            pltpu.VMEM((terms, sec, block, block), F32),
            pltpu.VMEM((sec, block, block), BF16),
            pltpu.VMEM((sec, block, block), BF16),
            pltpu.VMEM((slots, block, block), F32),
            pltpu.VMEM((sec, block, block), F32),
            pltpu.VMEM((sec, nx, rows, block), F32),
            pltpu.VMEM((sec, nx, rows, block), F32),
            pltpu.VMEM((sec, nx, rows, block), F32),
            dma((5,)),
            dma((nz, parts, nop)),
            dma((2, nz, parts)),
            dma((nz, parts, nx)),
            dma((nz, parts, nx)),
            dma((sec, nx)),
            dma((sec, nx)),
            dma((sec, nx)),
            dma((sec, nx)),
        ],
        compiler_params=pltpu.CompilerParams(
            collective_id=0, has_side_effects=True, vmem_limit_bytes=56 * 1024 * 1024
        ),
        cost_estimate=pl.CostEstimate(
            flops=12 * pairs * block ** 3, bytes_accessed=8 * pairs * block * block, transcendentals=0
        ),
    )(source.T, coef_index.T, coef_table, psi, left_env, right_env)


def solution(mesh):
    return jax.shard_map(
        functools.partial(on_device, mesh.shape["sector"], mesh.shape["op"]),
        mesh=mesh,
        in_specs=(
            P(("groups", "sector"), None, None),
            P("op", ("groups", "sector"), None, None),
            P("op", ("groups", "sector"), None, None),
            P(None, "groups"),
            P("op", ("groups", "sector")),
            P(),
        ),
        out_specs=P(("groups", "sector"), "op", None),
        check_vma=False,
    )
```

```python
import functools

import jax
import jax.numpy as jnp
from jax import lax
from jax.experimental import pallas as pl
from jax.experimental.pallas import tpu as pltpu
from jax.sharding import PartitionSpec as P

F32 = jnp.float32
BF16 = jnp.bfloat16
MESH = pl.DeviceIdType.MESH


def split(value):
    high = value.astype(BF16)
    return high, (value - high.astype(F32)).astype(BF16)


def dot3(a_hi, a_lo, b_hi, b_lo):
    dot = functools.partial(jnp.dot, preferred_element_type=F32)
    return dot(a_hi, b_hi) + dot(a_hi, b_lo) + dot(a_lo, b_hi)


def kernel(nz, nx, cap, parts, source_hbm, index_hbm, table_ref, psi_ref, left_ref, right_ref, out_ref,
           source_ref, index_ref, after, rank, reads, middle, psi_all, left, right, cur_hi, cur_lo, contrib, h, first, summed, second,
           load_sem, recv_sem, z_sem, x_sem, c_sem, r1_send, r1_recv, r2_send, r2_recv):
    sec = psi_ref.shape[0]
    block = psi_ref.shape[1]
    terms = left_ref.shape[0]
    nop = 2 * nx
    pairs = terms * sec
    rows = block // nop
    part = sec // parts
    z = lax.axis_index("sector")
    o = lax.axis_index("op")
    x = o // 2
    c = lax.rem(o, 2)
    mate = 2 * x + 1 - c

    load_psi = pltpu.make_async_copy(psi_ref, psi_all.at[z], load_sem.at[0])
    load_right = pltpu.make_async_copy(right_ref, right, load_sem.at[1])
    load_left = pltpu.make_async_copy(left_ref, left, load_sem.at[2])
    load_psi.start()
    load_source = pltpu.make_async_copy(source_hbm, source_ref, load_sem.at[3])
    load_index = pltpu.make_async_copy(index_hbm, index_ref, load_sem.at[4])
    load_source.start()
    load_index.start()

    def other(step):
        return lax.rem(x + step, nx)

    barrier = pltpu.get_barrier_semaphore()

    @pl.when(z > 0)
    def _():
        pl.semaphore_signal(barrier, inc=1, device_id={"sector": z - 1}, device_id_type=MESH)

    @pl.when(z < nz - 1)
    def _():
        pl.semaphore_signal(barrier, inc=1, device_id={"sector": z + 1}, device_id_type=MESH)

    pl.semaphore_signal(barrier, inc=1, device_id={"op": mate}, device_id_type=MESH)
    for step in range(1, nx):
        pl.semaphore_signal(barrier, inc=1, device_id={"op": 2 * other(step) + c}, device_id_type=MESH)

    inside = jnp.logical_and(z > 0, z < nz - 1)

    @pl.when(inside)
    def _():
        pl.semaphore_wait(barrier, nx + 2)

    @pl.when(jnp.logical_not(inside))
    def _():
        pl.semaphore_wait(barrier, nx + 1)

    def piece(k, i, q):
        return psi_all.at[k, pl.ds(i * part, part), pl.ds(pl.multiple_of(q * rows, rows), rows), :]

    def send(k, i, q, sem, device):
        return pltpu.make_async_remote_copy(
            src_ref=piece(k, i, q), dst_ref=piece(k, i, q), send_sem=sem, recv_sem=recv_sem.at[k, i, q],
            device_id=device, device_id_type=MESH)

    def z_copy(k, i, way):
        return send(k, i, o, z_sem.at[(way + 1) // 2, k, i], {"sector": z + way})

    def x_copy(k, i, step):
        return send(k, i, o, x_sem.at[k, i, step], {"op": 2 * other(step) + c})

    def c_copy(k, i, xq):
        return send(k, i, 2 * xq + c, c_sem.at[k, i, xq], {"op": mate})

    def arrived(k, i, q):
        send(k, i, q, z_sem.at[0, k, i], {"op": mate}).wait_recv()

    load_psi.wait()
    for i in range(parts):
        for way in (-1, 1):
            @pl.when(jnp.logical_and(z + way >= 0, z + way < nz))
            def _():
                z_copy(z, i, way).start()
    load_right.start()
    load_left.start()

    def source_of(p):
        return source_ref[z * sec + lax.rem(p, sec), o * terms + lax.div(p, sec)]

    load_source.wait()
    load_index.wait()

    def clear(p, carry):
        rank[p] = 0
        return carry
    lax.fori_loop(0, pairs, clear, 0)

    def chain(k):
        def backward(step, carry):
            found, count = carry
            p = pairs - 1 - step
            hit = lax.div(source_of(p), sec) == k
            after[p] = found
            rank[p] = jnp.where(hit, count, rank[p])
            return jnp.where(hit, p, found), jnp.where(hit, count + 1, count)
        found, count = lax.fori_loop(0, pairs, backward, (0, 0), unroll=True)
        reads[k] = count
        return found

    def slot(p):
        owner = lax.div(source_of(p), sec)
        return owner * cap + reads[owner] - 1 - rank[p]

    def ready(k):
        def halve(s, carry):
            cur_hi[s], cur_lo[s] = split(psi_all[k, s])
            return carry
        lax.fori_loop(0, sec, halve, 0, unroll=True)

    def products(k, begin, end, start):
        def pair(j, p):
            w = lax.div(p, sec)
            t = lax.rem(p, sec)
            s = lax.rem(source_of(p), sec)
            r_hi, r_lo = split(right[w, t])
            value = dot3(cur_hi[s], cur_lo[s], r_hi, r_lo) * table_ref[index_ref[t, w]]
            l_hi, l_lo = split(left[w, t])
            v_hi, v_lo = split(value)
            contrib[k * cap + j] = dot3(l_hi, l_lo, v_hi, v_lo)
            return after[p]
        return lax.fori_loop(begin, end, pair, start, unroll=True)

    ready(z)
    head = chain(z)
    def both(d, body):
        for side in (-1, 1):
            k = z + side * d
            @pl.when(jnp.logical_and(d >= 1, jnp.logical_and(d < nz, jnp.logical_and(k >= 0, k < nz))))
            def _():
                body(k, side)

    def take_z(i):
        def body(k, side):
            arrived(k, i, o)
            ahead = z - side

            @pl.when(jnp.logical_and(ahead >= 0, ahead < nz))
            def _():
                z_copy(k, i, -side).start()
            for step in range(1, nx):
                x_copy(k, i, step).start()
            c_copy(k, i, x).start()
        return body

    def take_x(i):
        def body(k, side):
            for step in range(1, nx):
                arrived(k, i, 2 * other(step) + c)
                c_copy(k, i, other(step)).start()
        return body

    def take_all(k, side):
        start = chain(k)
        for i in range(parts):
            for xq in range(nx):
                arrived(k, i, 2 * xq + 1 - c)
        ready(k)
        products(k, 0, cap, start)

    def stage(d, carry):
        for i in range(parts):
            both(d, take_z(i))

        @pl.when(d == 1)
        def _():
            load_right.wait()
            load_left.wait()
            middle[0] = products(z, 0, cap // 2, head)

        for i in range(parts):
            both(d - 1, take_x(i))

        @pl.when(d == 2)
        def _():
            products(z, cap // 2, cap, middle[0])
        both(d - 1, take_all)
        return carry
    lax.fori_loop(1, nz + 1, stage, 0)

    def mine(t, xq, core):
        return h.at[t, pl.ds(pl.multiple_of((2 * xq + core) * rows, rows), rows), :]

    def r1_copy(t, xq):
        return pltpu.make_async_remote_copy(
            src_ref=mine(t, xq, 1 - c), dst_ref=first.at[t, xq], send_sem=r1_send.at[t, xq],
            recv_sem=r1_recv.at[t, xq], device_id={"op": mate}, device_id_type=MESH)

    def r2_copy(t, step):
        return pltpu.make_async_remote_copy(
            src_ref=summed.at[t, other(step)], dst_ref=second.at[t, step], send_sem=r2_send.at[t, step],
            recv_sem=r2_recv.at[t, step], device_id={"op": 2 * other(step) + c}, device_id_type=MESH)

    def target(t, carry):
        @pl.when(t < sec)
        def _():
            at = [slot(w * sec + t) for w in range(terms)]

            def gather(xq, core):
                own = pl.ds(pl.multiple_of((2 * xq + core) * rows, rows), rows)
                total = contrib[at[0], own, :]
                for w in range(1, terms):
                    total = total + contrib[at[w], own, :]
                h[t, own, :] = total
            for xq in range(nx):
                gather(xq, 1 - c)
                r1_copy(t, xq).start()
            for xq in range(nx):
                gather(xq, c)

        @pl.when(t >= 1)
        def _():
            b = t - 1
            for xq in range(nx):
                r1_copy(b, xq).wait_recv()
                summed[b, xq] = mine(b, xq, c)[...] + first[b, xq]
            for step in range(1, nx):
                r2_copy(b, step).start()
        return carry
    lax.fori_loop(0, sec + 1, target, 0)

    def finish(t, carry):
        total = summed[t, x]
        for step in range(1, nx):
            r2_copy(t, step).wait_recv()
            total = total + second[t, step]
        out_ref[t] = total
        for step in range(1, nx):
            r2_copy(t, step).wait_send()
        for xq in range(nx):
            r1_copy(t, xq).wait_send()
        return carry
    lax.fori_loop(0, sec, finish, 0)

    for i in range(parts):
        for way in (-1, 1):
            @pl.when(jnp.logical_and(z + way >= 0, z + way < nz))
            def _():
                z_copy(z, i, way).wait_send()

    def drain(i):
        def body(k, side):
            ahead = z - side

            @pl.when(jnp.logical_and(ahead >= 0, ahead < nz))
            def _():
                z_copy(k, i, -side).wait_send()
            for step in range(1, nx):
                x_copy(k, i, step).wait_send()
            for xq in range(nx):
                c_copy(k, i, xq).wait_send()
        return body

    def last(d, carry):
        for i in range(parts):
            both(d, drain(i))
        return carry
    lax.fori_loop(1, nz, last, 0)


def on_device(nz, nop, psi, left_env, right_env, source, coef_index, coef_table):
    sec, block, _ = psi.shape
    terms = left_env.shape[0]
    pairs = terms * sec
    cap = -(-pairs // nz)
    slots = cap * nz
    nx = nop // 2
    rows = block // nop
    parts = 1
    dma = pltpu.SemaphoreType.DMA
    smem = pl.BlockSpec(memory_space=pltpu.SMEM)
    hbm = pl.BlockSpec(memory_space=pl.ANY)
    return pl.pallas_call(
        functools.partial(kernel, nz, nx, cap, parts),
        out_shape=jax.ShapeDtypeStruct((sec, rows, block), F32),
        in_specs=[hbm] * 2 + [smem] + [hbm] * 3,
        out_specs=pl.BlockSpec(memory_space=pltpu.VMEM),
        scratch_shapes=[
            pltpu.SMEM(source.shape[::-1], jnp.int32),
            pltpu.SMEM(coef_index.shape[::-1], jnp.int32),
            pltpu.SMEM((pairs,), jnp.int32),
            pltpu.SMEM((pairs,), jnp.int32),
            pltpu.SMEM((nz,), jnp.int32),
            pltpu.SMEM((1,), jnp.int32),
            pltpu.VMEM((nz, sec, block, block), F32),
            pltpu.VMEM((terms, sec, block, block), F32),
            pltpu.VMEM((terms, sec, block, block), F32),
            pltpu.VMEM((sec, block, block), BF16),
            pltpu.VMEM((sec, block, block), BF16),
            pltpu.VMEM((slots, block, block), F32),
            pltpu.VMEM((sec, block, block), F32),
            pltpu.VMEM((sec, nx, rows, block), F32),
            pltpu.VMEM((sec, nx, rows, block), F32),
            pltpu.VMEM((sec, nx, rows, block), F32),
            dma((5,)),
            dma((nz, parts, nop)),
            dma((2, nz, parts)),
            dma((nz, parts, nx)),
            dma((nz, parts, nx)),
            dma((sec, nx)),
            dma((sec, nx)),
            dma((sec, nx)),
            dma((sec, nx)),
        ],
        compiler_params=pltpu.CompilerParams(
            collective_id=0, has_side_effects=True, vmem_limit_bytes=56 * 1024 * 1024
        ),
        cost_estimate=pl.CostEstimate(
            flops=12 * pairs * block ** 3, bytes_accessed=8 * pairs * block * block, transcendentals=0
        ),
    )(source.T, coef_index.T, coef_table, psi, left_env, right_env)


def solution(mesh):
    return jax.shard_map(
        functools.partial(on_device, mesh.shape["sector"], mesh.shape["op"]),
        mesh=mesh,
        in_specs=(
            P(("groups", "sector"), None, None),
            P("op", ("groups", "sector"), None, None),
            P("op", ("groups", "sector"), None, None),
            P(None, "groups"),
            P("op", ("groups", "sector")),
            P(),
        ),
        out_specs=P(("groups", "sector"), "op", None),
        check_vma=False,
    )
```
